32 devices in a mesh: groups: 2 (over x), sect: 8 (over z, y), tp: 2 (over core).
Axes of the slice: x: 2, y: 2, z: 4, core: 2. Of those that a mesh axis runs over, the one named last changes fastest.
Arguments:
- queries: bfloat16 [512, 64, 128], P(('groups', 'sect'), 'tp'), parts along dimension 0, may hold values from -23 to 23
- keys: bfloat16 [512, 128, 2, 128], P(('groups', 'sect'), None, 'tp'), parts along dimension 0, may hold values from -4 to 4
- values: bfloat16 [512, 128, 2, 128], P(('groups', 'sect'), None, 'tp'), parts along dimension 0, may hold values from -12 to 12
- kv_lengths: int32 [512], P(('groups', 'sect')), parts along dimension 0, may hold values from 2 to 128, as said below
- out_proj: bfloat16 [8192, 3584], P('tp', 'sect'), may hold values from -0.0625 to 0.0625
- resid: bfloat16 [512, 3584], P(('groups', 'sect')), parts along dimension 0, may hold values from -6 to 6
- norm_gain: bfloat16 [3584], replicated, may hold values from 0.099609375 to 1.8984375
- experts_chosen: int32 [512, 3], P(('groups', 'sect')), parts along dimension 0, may hold values from 0 to 7, all different within a row; in each aligned block of 32 rows (0 to 31, 32 to 63, ...) at most 16 rows name the same one
- route_probs: float32 [512, 3], P(('groups', 'sect')), parts along dimension 0, may hold values from 0.1 to 1
- expert_home: int32 [8], replicated, may hold values from 0 to 7, each once
- gate_up: bfloat16 [2, 3584, 20480], P(None, None, ('sect', 'tp')), may hold values from -0.09375 to 0.09375
- down_proj: bfloat16 [20480, 3584], P(('sect', 'tp')), may hold values from -0.125 to 0.125
Outputs:
- layer_out: bfloat16 [512, 3584], P(('groups', 'sect'), 'tp'), parts along dimension 0
The draws below stay inside these ranges and needn't reach their ends.
There are 2 independent parts, one for each index of `groups`. The reference program is written for one: setup_inputs(seed, part) draws one part's arguments, and reference() takes and returns one part's arrays. A program takes and returns all parts, laid end to end along the dimension named above; an argument that names none is the same for every part. Nothing has to cross between parts.
Inputs may be any that keep to these rules, and one draw needn't show every extreme that they name: `experts_chosen`: each request names 3 different experts; among the 32 requests of one index of sect no expert is named more than 16 times, a bound that some block reaches there. `expert_home`: each band is named once. `kv_lengths`: in every aligned block of 32 requests some request uses all 128 positions.
All inputs are finite; a program needn't handle non-finite values.
Results may differ from the reference program's by a relative error of at most 0.0058.
Values may be sent and summed in bfloat16 or wider, within the bound.
A program may use at most 128 MiB of HBM per device.

```python
import math
import jax
import jax.numpy as jnp
import numpy as np
from jax import lax

D = 3584
HEADS = 64
KV_HEADS = 2
HEAD_DIM = 128
EXP_HID = 2560
EXPERTS = 8
TOPK = 3
CTX = 128
ROWS_DEV = 32
ROWS = 256
HID_DEV = 1280
CAP = 16
GROUP = 32


def key_base(key):
    first_key = jax.random.fold_in(key, 0)
    normal_part = jnp.clip(jax.random.normal(first_key, (ROWS, CTX, KV_HEADS, HEAD_DIM), jnp.float32), -4.0, 4.0)
    return normal_part


def draw_keys(key, part):
    normal_part = key_base(key)
    cached = normal_part
    return cached.astype(jnp.bfloat16)


def draw_queries(key, part):
    key = jax.random.fold_in(key, 5)
    drawn_queries = jnp.clip(jax.random.normal(key, (ROWS, HEADS, HEAD_DIM), jnp.float32), -4.0, 4.0)
    return drawn_queries.astype(jnp.bfloat16)


def draw_kv_lengths(key, part):
    key = jax.random.fold_in(key, 7)
    drawn_lengths = jax.random.randint(key, (ROWS,), 2, CTX + 1)
    row_ids = jnp.arange(ROWS, dtype=jnp.int32)
    return jnp.where(row_ids % ROWS_DEV == 0, CTX, drawn_lengths).astype(jnp.int32)


def block_scale(own_key, dims, shards, least, high):
    level, own = 1.0, jax.random.fold_in(own_key, 6)
    for dim, blocks in shards:
        steps = jnp.exp(jax.random.uniform(jax.random.fold_in(own, dim), (blocks,), jnp.float32, least / len(shards), high / len(shards)))
        level = level * jnp.repeat(steps, dims[dim] // blocks).reshape([-1 if axis == dim else 1 for axis in range(len(dims))])
    return level


def assign_block(stream_key, own, number, rows, number_of, top, reach, skew):
    sequence = jax.random.permutation(stream_key, number_of)
    crowded, usual = portions_of(number_of, rows * top, reach, skew, True), portions_of(number_of, rows * top, reach, skew, False)
    places = jnp.arange(number_of)

    def named(tallies, offset_by):
        used = int((tallies > 0).sum())
        fixed = max(1, used // 4)
        passed = fixed + (places - fixed + offset_by * (used - fixed)) % max(1, number_of - fixed)
        return jnp.zeros((number_of,), jnp.int32).at[sequence[jnp.where(places < fixed, places, passed)]].set(jnp.asarray(tallies, jnp.int32))

    tallies = jnp.where(number % 4 == 0, named(crowded, number // 4), named(usual, number - number // 4 - 1))
    mixed = jax.random.permutation(jax.random.fold_in(own, 3), number_of)
    source_of, sink = mixed[0:number_of // 2 * 2:2], mixed[1:number_of // 2 * 2:2]
    room = jnp.minimum(tallies[source_of] - 1, reach - tallies[sink]) // 2
    room = jnp.where((source_of == sequence[0]) | (sink == sequence[0]) | (tallies[sink] == 0), 0, jnp.maximum(room, 0))
    passed = jax.random.randint(jax.random.fold_in(own, 4), (number_of // 2,), 0, 1 << 20) % (room + 1)
    tallies = tallies.at[source_of].add(-passed).at[sink].add(passed)
    labels = jnp.searchsorted(jnp.cumsum(tallies), jnp.arange(rows * top), side="right").astype(jnp.int32)
    grid = labels.reshape(top, rows).T
    grid = grid[jax.random.permutation(jax.random.fold_in(own, 1), rows)]
    offset_by = jax.random.randint(jax.random.fold_in(own, 2), (rows, 1), 0, top)
    return jnp.take_along_axis(grid, (jnp.arange(top)[None, :] + offset_by) % top, axis=1)


def portions_of(amount, total, bound, lean, full):
    loads = [(1 << 20) // math.isqrt(rank ** lean) + 1 for rank in range(1, amount + 1)]
    largest = bound if full else min(bound, max(-(-total // amount), total * loads[0] // sum(loads)))
    least = 1 if total - largest >= amount - 1 else 0
    given, surplus = [largest] + [least] * (amount - 1), total - largest - least * (amount - 1)
    while surplus > 0:
        free = [i for i in range(1, amount) if given[i] < largest] or [i for i in range(1, amount) if given[i] < bound]
        pool, remaining = sum([loads[i] for i in free]), surplus
        for i in free:
            extra = min(bound - given[i], max(1, remaining * loads[i] // pool), surplus)
            given[i] = given[i] + extra
            surplus = surplus - extra
    return np.array(given)


def normal_values(stream_key, dims, scale, bound, cuts=(), held_as=jnp.bfloat16):
    gain = block_scale(stream_key, dims, cuts, -0.22, 0.18) if cuts else 1.0
    drawn = jax.random.normal(stream_key, dims, jnp.float32) * scale * gain
    return jnp.minimum(jnp.maximum(drawn, -bound), bound).astype(held_as)


def setup_inputs(seed: int = 0, part: int = 0) -> dict:
    key_of = jax.random.split(jax.random.key(seed), 13)
    own_keys = jax.random.split(jax.random.fold_in(key_of[12], part), 13)
    queries = draw_queries(jax.random.fold_in(jax.random.fold_in(key_of[12], part), 71), part)
    keys = draw_keys(jax.random.fold_in(jax.random.fold_in(key_of[12], part), 71), part)
    values = normal_values(own_keys[2], (ROWS, CTX, KV_HEADS, HEAD_DIM), 2.0, 12.0, ((0, 8), (2, 2)))
    kv_lengths = draw_kv_lengths(jax.random.fold_in(jax.random.fold_in(key_of[12], part), 71), part)
    out_proj = normal_values(key_of[4], (HEADS * HEAD_DIM, D), (HEADS * HEAD_DIM) ** -0.5, 0.0625, ((0, 2), (1, 8)))
    resid = normal_values(own_keys[5], (ROWS, D), 1.0, 6.0, ((0, 8),))
    norm_gain = jnp.clip(1.0 + 0.18 * jax.random.normal(key_of[6], (D,), jnp.float32), 0.099609375, 1.8984375).astype(jnp.bfloat16)
    experts_chosen_keys = jax.random.split(jax.random.fold_in(own_keys[7], 1), ROWS // ROWS_DEV)
    experts_chosen_turns = jax.random.permutation(jax.random.fold_in(own_keys[7], 3), ROWS // ROWS_DEV)
    experts_chosen = jax.vmap(lambda own, number: assign_block(jax.random.fold_in(own_keys[7], 2), own, number, ROWS_DEV, EXPERTS, TOPK, CAP, 2))(experts_chosen_keys, experts_chosen_turns).reshape((ROWS, TOPK))
    route_probs = jnp.clip(0.1 + 0.9 * jax.random.uniform(own_keys[8], (ROWS, TOPK), jnp.float32) ** block_scale(own_keys[8], (ROWS, TOPK), ((0, 8),), -0.2, 0.2), 0.1, 1.0)
    expert_home = jax.random.permutation(key_of[9], EXPERTS).astype(jnp.int32)
    gate_up = normal_values(key_of[10], (2, D, EXPERTS * EXP_HID), D ** -0.5, 0.09375, ((2, 16),))
    down_proj = normal_values(key_of[11], (EXPERTS * EXP_HID, D), EXP_HID ** -0.5, 0.125, ((0, 16),))
    return dict(queries=queries, keys=keys, values=values, kv_lengths=kv_lengths, out_proj=out_proj, resid=resid, norm_gain=norm_gain, experts_chosen=experts_chosen, route_probs=route_probs, expert_home=expert_home, gate_up=gate_up, down_proj=down_proj)


def reference(queries, keys, values, kv_lengths, out_proj, resid, norm_gain, experts_chosen, route_probs, expert_home, gate_up, down_proj):
    grouped = queries.astype(jnp.float32).reshape(ROWS, KV_HEADS, GROUP, HEAD_DIM)
    scores = jnp.einsum('rkgd,rckd->rkgc', grouped, keys.astype(jnp.float32)) / math.sqrt(HEAD_DIM)
    visible = (jnp.arange(CTX, dtype=jnp.int32)[None, :] < kv_lengths[:, None])[:, None, None, :]
    scores = jnp.where(visible, scores, -1e+30)
    row_peak = lax.optimization_barrier(jnp.max(scores, axis=-1, keepdims=True))
    exponent = jnp.where(visible, jnp.exp(scores - row_peak), 0.0)
    weights = (exponent / lax.optimization_barrier(jnp.sum(exponent, axis=-1, keepdims=True))).astype(jnp.bfloat16)
    weights = lax.optimization_barrier(weights).astype(jnp.float32)
    heads_out = jnp.einsum('rkgc,rckd->rkgd', weights, values.astype(jnp.float32)).astype(jnp.bfloat16)
    heads_out = heads_out.reshape(ROWS, HEADS * HEAD_DIM)
    attended = resid.astype(jnp.float32) + jnp.dot(heads_out, out_proj, preferred_element_type=jnp.float32)
    mean_square = lax.optimization_barrier(jnp.mean(attended * attended, axis=-1, keepdims=True))
    normed = (attended * lax.rsqrt(mean_square + 1e-06) * norm_gain.astype(jnp.float32)).astype(jnp.bfloat16)
    blocks = EXP_HID // HID_DEV

    def one_expert(expert_id):
        col_start = (expert_home[expert_id] * EXP_HID).astype(jnp.int32)
        gate_cols = lax.dynamic_slice_in_dim(gate_up[0], col_start, EXP_HID, 1)
        up_cols = lax.dynamic_slice_in_dim(gate_up[1], col_start, EXP_HID, 1)
        down_rows = lax.dynamic_slice_in_dim(down_proj, col_start, EXP_HID, 0)
        gate_value = jnp.dot(normed, gate_cols, preferred_element_type=jnp.float32)
        up_value = jnp.dot(normed, up_cols, preferred_element_type=jnp.float32)
        activated = (jax.nn.silu(gate_value) * up_value).astype(jnp.bfloat16)
        activated = lax.optimization_barrier(activated).astype(jnp.float32).reshape(ROWS, blocks, HID_DEV)
        down_blocks = down_rows.astype(jnp.float32).reshape(blocks, HID_DEV, D)
        partial_value = jnp.einsum('rjh,jhd->rjd', activated, down_blocks).astype(jnp.bfloat16)
        partial_value = lax.optimization_barrier(partial_value).astype(jnp.float32)
        expert_out = lax.optimization_barrier(jnp.sum(partial_value, axis=1))
        weight = lax.optimization_barrier(jnp.sum(jnp.where(experts_chosen == expert_id, route_probs, 0.0), axis=1))
        return weight[:, None] * expert_out

    def accumulate(expert_id, total):
        return total + one_expert(expert_id)
    expert_sum = lax.fori_loop(0, EXPERTS, accumulate, jnp.zeros((ROWS, D), jnp.float32))
    return (attended + expert_sum).astype(jnp.bfloat16)
```

```python
import functools
import math

import jax
import jax.numpy as jnp
from jax import lax
from jax.experimental import pallas as pl
from jax.experimental.pallas import tpu as pltpu
from jax.sharding import PartitionSpec as P

CAP_SHARE = 2


def each(count, start, f):
    if count <= 8:
        for i in range(start, count):
            f(i)
    else:

        def step(i, carry):
            f(i)
            return carry

        lax.fori_loop(start, count, step, 0)


def layer_kernel(
    S,
    NC,
    NR,
    heads,
    wo_hbm,
    resid,
    gain,
    selector,
    mixing,
    wg_hbm,
    wd_hbm,
    att_out,
    es_out,
    wo,
    wg,
    wd,
    gath,
    part,
    tp_in,
    feat_out,
    feat_in,
    normed,
    attended,
    packed,
    xbuf,
    acc,
    act,
    down_out,
    down_in,
    ret_out,
    ret_in,
    w_sem,
    ring_send,
    ring_recv,
    tpx_send,
    tpx_recv,
    feat_send,
    feat_recv,
    nx_send,
    nx_recv,
    disp_send,
    disp_recv,
    share_send,
    share_recv,
    dx_send,
    dx_recv,
    ret_send,
    ret_recv,
):
    f32, bf16 = jnp.float32, jnp.bfloat16
    s = lax.axis_index("sect")
    t = lax.axis_index("tp")
    rows, heads_width = heads.shape
    half = rows // 2
    F = wo.shape[1]
    D = F * S
    cap = xbuf.shape[1] // S
    HB = S // 2
    CB = HB // NC
    W = ret_in.shape[2]
    ring_half = S // 2

    def ring_index(q):
        return jnp.where(q < ring_half, 2 * q, 2 * (S - 1 - q) + 1)

    pos = jnp.where(s % 2 == 0, s // 2, S - 1 - (s - 1) // 2)

    def owner(rel):
        return ring_index((pos + rel + S) % S)

    right, left = owner(1), owner(-1)

    def remote(src, dst, ss, rs, **dev):
        return pltpu.make_async_remote_copy(
            src_ref=src,
            dst_ref=dst,
            send_sem=ss,
            recv_sem=rs,
            device_id=dev,
            device_id_type=pl.DeviceIdType.MESH,
        )

    copies = [
        pltpu.make_async_copy(wo_hbm, wo, w_sem.at[0]),
        pltpu.make_async_copy(wg_hbm.at[0], wg.at[0], w_sem.at[1]),
        pltpu.make_async_copy(wg_hbm.at[1], wg.at[1], w_sem.at[2]),
        pltpu.make_async_copy(wd_hbm, wd, w_sem.at[3]),
    ]
    for c in copies:
        c.start()

    barrier = pltpu.get_barrier_semaphore()
    pl.semaphore_signal(
        barrier, inc=1, device_id={"tp": 1 - t}, device_id_type=pl.DeviceIdType.MESH
    )

    def greet(d):
        pl.semaphore_signal(
            barrier,
            inc=1,
            device_id={"sect": (s + d) % S},
            device_id_type=pl.DeviceIdType.MESH,
        )

    each(S, 1, greet)
    pl.semaphore_wait(barrier, S)

    def slot(k, direction):
        if k == 0:
            return 0
        return 2 * k - 1 if direction == 0 or k == ring_half else 2 * k

    def ring_copy(k, direction, h):
        src_row = slot(k - 1, direction) * rows + h * half
        dst_row = slot(k, direction) * rows + h * half
        src = heads.at[pl.ds(h * half, half)] if k == 1 else gath.at[pl.ds(src_row, half)]
        return remote(
            src,
            gath.at[pl.ds(dst_row, half)],
            ring_send.at[direction, k - 1, h],
            ring_recv.at[direction, k - 1, h],
            sect=right if direction == 0 else left,
        )

    def ring_pairs(k):
        return [(0, 0), (1, 1)] if k == ring_half else [(0, 0), (1, 0), (0, 1), (1, 1)]

    for direction, h in [(0, 0), (1, 1), (0, 1), (1, 0)]:
        ring_copy(1, direction, h).start()

    def exchange(o):
        return remote(
            part.at[o, 1 - t],
            tp_in.at[o],
            tpx_send.at[o],
            tpx_recv.at[o],
            tp=1 - t,
        )

    def rel_of(o):
        if o == 0:
            return 0
        k = (o + 1) // 2
        return -k if o % 2 == 1 else k

    def feature_copy(o):
        return remote(
            feat_out.at[o],
            feat_in.at[s],
            feat_send.at[o],
            feat_recv.at[s],
            sect=owner(rel_of(o)),
        )

    def feature_arrival(j):
        return remote(feat_out.at[0], feat_in.at[j], feat_send.at[0], feat_recv.at[j], sect=j)

    def finish(o):
        exchange(o).wait_recv()
        total = part[o, t] + tp_in[o]
        if o == 0:
            feat_in[s] = total.astype(bf16)
        else:
            feat_out[o] = total.astype(bf16)
            feature_copy(o).start()

    def project(block, first, count):
        product = jnp.dot(block, wo[...], preferred_element_type=f32)
        for b in range(count):
            for h in range(2):
                part[first + b, h] = product[b * rows + h * half : b * rows + (h + 1) * half]
            exchange(first + b).start()

    copies[0].wait()
    project(heads[...], 0, 1)
    waiting = [0]
    for k in range(1, ring_half + 1):
        for direction, h in ring_pairs(k):
            ring_copy(k, direction, h).wait_recv()
            if k < ring_half and (direction, h) in ring_pairs(k + 1):
                ring_copy(k + 1, direction, h).start()
        if k < ring_half:
            project(gath[pl.ds((2 * k - 1) * rows, 2 * rows)], 2 * k - 1, 2)
            for o in waiting:
                finish(o)
            waiting = [2 * k - 1, 2 * k]
        else:
            project(gath[pl.ds((S - 1) * rows, rows)], S - 1, 1)
            for o in waiting:
                finish(o)
            finish(S - 1)

    def await_features(d):
        feature_arrival((s + d) % S).wait_recv()

    each(S, 1, await_features)
    squares = jnp.zeros((half, 1), f32)
    for j in range(S):
        a = resid[t, j].astype(f32) + feat_in[j].astype(f32)
        attended[t, j] = a
        squares = squares + jnp.sum(a * a, axis=1, keepdims=True)
    scale = lax.rsqrt(squares * (1.0 / D) + 1e-06)
    for j in range(S):
        normed[t, j] = (attended[t, j] * scale * gain[j].astype(f32)).astype(bf16)
    normed_copy = remote(normed.at[t], normed.at[t], nx_send.at[0], nx_recv.at[0], tp=1 - t)
    normed_copy.start()
    theirs = pl.ds((1 - t) * HB, HB)
    att_copy = remote(
        attended.at[t, theirs], attended.at[t, theirs], nx_send.at[1], nx_recv.at[1], tp=1 - t
    )
    att_copy.start()
    normed_arrival = remote(
        normed.at[1 - t], normed.at[1 - t], nx_send.at[0], nx_recv.at[0], tp=1 - t
    )
    normed_arrival.wait_recv()

    mine = pl.ds(s * cap, cap)

    def dispatch_copy(c, d):
        dest = (s + d) % S
        return remote(
            packed.at[pl.ds(c * CB, CB), pl.ds(dest * cap, cap)],
            xbuf.at[pl.ds(t * HB + c * CB, CB), mine],
            disp_send.at[c, d],
            disp_recv.at[c, d],
            sect=dest,
        )

    def dispatch_arrival(c, d):
        sender = (s - d + S) % S
        return remote(
            packed.at[pl.ds(c * CB, CB), pl.ds(sender * cap, cap)],
            xbuf.at[pl.ds(t * HB + c * CB, CB), pl.ds(sender * cap, cap)],
            disp_send.at[c, d],
            disp_recv.at[c, d],
            sect=sender,
        )

    def share_copy(c, core):
        blocks = xbuf.at[pl.ds(core * HB + c * CB, CB)]
        return remote(blocks, blocks, share_send.at[c], share_recv.at[c], tp=1 - t)

    sel = selector[...]
    for c in range(NC):
        for b in range(CB):
            i = c * CB + b
            j = t * HB + i
            block = jnp.concatenate([normed[0, j], normed[1, j]], axis=0)
            packed[i] = jnp.dot(sel, block, preferred_element_type=f32).astype(bf16)
            xbuf[j, mine] = packed[i, mine]
        each(S, 1, lambda d: dispatch_copy(c, d).start())

    copies[1].wait()
    copies[2].wait()

    def accumulate(c, core):
        for b in range(CB):
            j = core * HB + c * CB + b
            x = xbuf[j]
            k_rows = pl.ds(pl.multiple_of(j * F, 16), F)
            for m in range(2):
                acc[m] += jnp.dot(x, wg[m, k_rows, :], preferred_element_type=f32)

    acc[...] = jnp.zeros_like(acc)
    for c in range(NC):
        each(S, 1, lambda d: dispatch_arrival(c, d).wait_recv())
        share_copy(c, t).start()
        accumulate(c, t)
        if c > 0:
            share_copy(c - 1, 1 - t).wait_recv()
            accumulate(c - 1, 1 - t)
    share_copy(NC - 1, 1 - t).wait_recv()
    accumulate(NC - 1, 1 - t)

    gate_value = acc[0]
    act[...] = (gate_value / (1.0 + jnp.exp(-gate_value)) * acc[1]).astype(bf16)
    copies[3].wait()

    def down_columns(core, r):
        return pl.ds(pl.multiple_of(core * (NR * W) + r * W, 128), W)

    def down_copy(r):
        return remote(down_out.at[r], down_in.at[r], dx_send.at[r], dx_recv.at[r], tp=1 - t)

    def return_copy(r, d):
        dest = (s + d) % S
        return remote(
            ret_out.at[r, pl.ds(dest * cap, cap)],
            ret_in.at[r, mine],
            ret_send.at[r, d],
            ret_recv.at[r, d],
            sect=dest,
        )

    def return_arrival(r, d):
        rows_of = pl.ds(((s - d + S) % S) * cap, cap)
        return remote(
            ret_out.at[r, rows_of],
            ret_in.at[r, rows_of],
            ret_send.at[r, d],
            ret_recv.at[r, d],
            sect=(s - d + S) % S,
        )

    for r in range(NR):
        down_out[r] = jnp.dot(
            act[...], wd[:, down_columns(1 - t, r)], preferred_element_type=f32
        ).astype(bf16)
        down_copy(r).start()
        own = jnp.dot(
            act[...], wd[:, down_columns(t, r)], preferred_element_type=f32
        ).astype(bf16)
        down_copy(r).wait_recv()
        ret_out[r] = (own.astype(f32) + down_in[r].astype(f32)).astype(bf16)
        each(S, 1, lambda d: return_copy(r, d).start())
        ret_in[r, mine] = ret_out[r, mine]

    mix = mixing[...]
    mix_high = mix.astype(bf16)
    rest = mix - mix_high.astype(f32)
    mix_mid = rest.astype(bf16)
    mix_low = (rest - mix_mid.astype(f32)).astype(bf16)

    att_arrival = remote(
        attended.at[1 - t, pl.ds(t * HB, HB)],
        attended.at[1 - t, pl.ds(t * HB, HB)],
        nx_send.at[1],
        nx_recv.at[1],
        tp=1 - t,
    )
    att_arrival.wait_recv()
    for h in range(2):
        att_out[h] = attended[h, pl.ds(t * HB, HB)]
    for r in range(NR):
        each(S, 1, lambda d: return_arrival(r, d).wait_recv())
        got = ret_in[r]
        es_out[:, r * W : (r + 1) * W] = (
            jnp.dot(mix_high, got, preferred_element_type=f32)
            + jnp.dot(mix_mid, got, preferred_element_type=f32)
            + jnp.dot(mix_low, got, preferred_element_type=f32)
        )

    for k in range(1, ring_half + 1):
        for direction, h in ring_pairs(k):
            ring_copy(k, direction, h).wait_send()
    for o in range(S):
        exchange(o).wait_send()
        if o > 0:
            feature_copy(o).wait_send()
    normed_copy.wait_send()
    att_copy.wait_send()
    for c in range(NC):
        each(S, 1, lambda d: dispatch_copy(c, d).wait_send())
        share_copy(c, t).wait_send()
    for r in range(NR):
        down_copy(r).wait_send()
        each(S, 1, lambda d: return_copy(r, d).wait_send())


def layer_call(S, heads, out_proj, resid, gain, selector, mixing, gate_up, down_proj):
    f32, bf16 = jnp.float32, jnp.bfloat16
    rows, heads_width = heads.shape
    half = rows // 2
    F = out_proj.shape[1]
    D = F * S
    hidden = down_proj.shape[0]
    slots = selector.shape[0]
    HB = S // 2
    NC = math.gcd(HB, 4)
    NR = 2
    W = D // 2 // NR
    dma = pltpu.SemaphoreType.DMA
    vmem = pl.BlockSpec(memory_space=pltpu.VMEM)
    hbm = pl.BlockSpec(memory_space=pl.ANY)
    return pl.pallas_call(
        functools.partial(layer_kernel, S, NC, NR),
        out_shape=(
            jax.ShapeDtypeStruct((2, HB, half, F), f32),
            jax.ShapeDtypeStruct((rows, D // 2), f32),
        ),
        in_specs=[vmem, hbm, vmem, vmem, vmem, vmem, hbm, hbm],
        out_specs=(vmem, vmem),
        scratch_shapes=[
            pltpu.VMEM(out_proj.shape, bf16),
            pltpu.VMEM(gate_up.shape, bf16),
            pltpu.VMEM(down_proj.shape, bf16),
            pltpu.VMEM((S * rows, heads_width), bf16),
            pltpu.VMEM((S, 2, half, F), f32),
            pltpu.VMEM((S, half, F), f32),
            pltpu.VMEM((S, half, F), bf16),
            pltpu.VMEM((S, half, F), bf16),
            pltpu.VMEM((2, S, half, F), bf16),
            pltpu.VMEM((2, S, half, F), f32),
            pltpu.VMEM((HB, slots, F), bf16),
            pltpu.VMEM((S, slots, F), bf16),
            pltpu.VMEM((2, slots, hidden), f32),
            pltpu.VMEM((slots, hidden), bf16),
            pltpu.VMEM((NR, slots, W), bf16),
            pltpu.VMEM((NR, slots, W), bf16),
            pltpu.VMEM((NR, slots, W), bf16),
            pltpu.VMEM((NR, slots, W), bf16),
            dma((4,)),
            dma((2, S // 2, 2)),
            dma((2, S // 2, 2)),
            dma((S,)),
            dma((S,)),
            dma((S,)),
            dma((S,)),
            dma((2,)),
            dma((2,)),
            dma((NC, S)),
            dma((NC, S)),
            dma((NC,)),
            dma((NC,)),
            dma((NR,)),
            dma((NR,)),
            dma((NR, S)),
            dma((NR, S)),
        ],
        compiler_params=pltpu.CompilerParams(
            collective_id=0, has_side_effects=True, vmem_limit_bytes=56 * 1024 * 1024
        ),
        cost_estimate=pl.CostEstimate(
            flops=2 * S * rows * heads_width * F + 6 * slots * D * hidden,
            bytes_accessed=2 * (out_proj.size + gate_up.size + down_proj.size),
            transcendentals=slots * hidden,
        ),
    )(heads, out_proj, resid, gain, selector, mixing, gate_up, down_proj)


def body(
    queries,
    keys,
    values,
    kv_lengths,
    out_proj,
    resid,
    norm_gain,
    experts_chosen,
    route_probs,
    expert_home,
    gate_up,
    down_proj,
):
    row_count, local_heads, head_dim = queries.shape
    context = keys.shape[1]
    local_kv = keys.shape[2]
    width = resid.shape[1]
    experts = expert_home.shape[0]
    top_count = experts_chosen.shape[1]
    S = lax.axis_size("sect")
    half = row_count // 2
    F = width // S
    band_size = S // experts
    capacity = row_count // CAP_SHARE

    grouped = queries.reshape(row_count, local_kv, local_heads // local_kv, head_dim)
    scores = jnp.einsum(
        "rkgd,rckd->rkgc", grouped, keys, preferred_element_type=jnp.float32
    ) / math.sqrt(head_dim)
    visible = (jnp.arange(context, dtype=jnp.int32)[None, :] < kv_lengths[:, None])[
        :, None, None, :
    ]
    scores = jnp.where(visible, scores, -1e30)
    row_peak = jnp.max(scores, axis=-1, keepdims=True)
    exponent = jnp.where(visible, jnp.exp(scores - row_peak), 0.0)
    weights = (exponent / jnp.sum(exponent, axis=-1, keepdims=True)).astype(jnp.bfloat16)
    heads_out = jnp.einsum(
        "rkgc,rckd->rkgd", weights, values, preferred_element_type=jnp.float32
    ).astype(jnp.bfloat16)
    heads_out = heads_out.reshape(row_count, local_heads * head_dim)

    chosen_flat = experts_chosen.reshape(-1)
    matches = (chosen_flat[:, None] == jnp.arange(experts, dtype=jnp.int32)[None, :]).astype(
        jnp.int32
    )
    earlier = jnp.cumsum(matches, axis=0) - matches
    slot_index = jnp.sum(earlier * matches, axis=1)
    home_band = jnp.sum(matches * expert_home[None, :], axis=1)
    position = (home_band * capacity + slot_index).reshape(row_count, top_count)
    table = jnp.arange(S * capacity, dtype=jnp.int32)
    table = (table // capacity) // band_size * capacity + table % capacity
    hits = position[:, :, None] == table[None, None, :]
    selector = jnp.any(hits, axis=1).T.astype(jnp.bfloat16)
    mixing = jnp.sum(jnp.where(hits, route_probs[:, :, None], 0.0), axis=1)

    resid_blocks = resid.reshape(2, half, S, F).transpose(0, 2, 1, 3)
    gain_blocks = norm_gain.reshape(S, 1, F)
    att, expert_sum = layer_call(
        S, heads_out, out_proj, resid_blocks, gain_blocks, selector, mixing, gate_up, down_proj
    )
    att = att.transpose(0, 2, 1, 3).reshape(row_count, width // 2)
    return (att + expert_sum).astype(jnp.bfloat16)


def solution(mesh):
    in_specs = (
        P(("groups", "sect"), "tp", None),
        P(("groups", "sect"), None, "tp", None),
        P(("groups", "sect"), None, "tp", None),
        P(("groups", "sect")),
        P("tp", "sect"),
        P(("groups", "sect"), None),
        P(),
        P(("groups", "sect"), None),
        P(("groups", "sect"), None),
        P(),
        P(None, None, ("sect", "tp")),
        P(("sect", "tp"), None),
    )
    out_specs = P(("groups", "sect"), "tp")
    return jax.shard_map(body, mesh=mesh, in_specs=in_specs, out_specs=out_specs, check_vma=False)
```

```python
import functools
import math

import jax
import jax.numpy as jnp
from jax import lax
from jax.experimental import pallas as pl
from jax.experimental.pallas import tpu as pltpu
from jax.sharding import PartitionSpec as P

CAP_SHARE = 2


def each(count, start, f):
    if count <= 8:
        for i in range(start, count):
            f(i)
    else:

        def step(i, carry):
            f(i)
            return carry

        lax.fori_loop(start, count, step, 0)


def layer_kernel(
    S,
    widths,
    lengths,
    home,
    q_hbm,
    k_hbm,
    v_hbm,
    wo_hbm,
    resid,
    gain,
    chosen,
    probs,
    wg_hbm,
    wd_hbm,
    out,
    q,
    kc,
    vc,
    wo,
    wg,
    wd,
    attn,
    gath,
    part,
    tp_in,
    feat_out,
    feat_in,
    normed,
    attended,
    selector,
    mixing,
    packed,
    xbuf,
    acc,
    act,
    down_out,
    down_in,
    ret_out,
    ret_in,
    kv_sem,
    w_sem,
    ring_send,
    ring_recv,
    tpx_send,
    tpx_recv,
    feat_send,
    feat_recv,
    nx_send,
    nx_recv,
    disp_send,
    disp_recv,
    share_send,
    share_recv,
    dx_send,
    dx_recv,
    ret_send,
    ret_recv,
):
    f32, bf16 = jnp.float32, jnp.bfloat16
    s = lax.axis_index("sect")
    t = lax.axis_index("tp")
    rows, heads_count, head_dim = q.shape
    context = kc.shape[1]
    half = rows // 2
    F = wo.shape[0]
    D = F * S
    H = D // 2
    cap = xbuf.shape[0] // S
    experts = home.shape[0]
    band_size = S // experts
    top_count = chosen.shape[0]
    NC = len(widths)
    starts = [sum(widths[:c]) for c in range(NC)]
    ring_half = S // 2

    def ring_index(p):
        return jnp.where(p < ring_half, 2 * p, 2 * (S - 1 - p) + 1)

    pos = jnp.where(s % 2 == 0, s // 2, S - 1 - (s - 1) // 2)

    def owner(rel):
        return ring_index((pos + rel + S) % S)

    right, left = owner(1), owner(-1)

    def remote(src, dst, ss, rs, **dev):
        return pltpu.make_async_remote_copy(
            src_ref=src,
            dst_ref=dst,
            send_sem=ss,
            recv_sem=rs,
            device_id=dev,
            device_id_type=pl.DeviceIdType.MESH,
        )

    kv_copies = []
    for h in range(2):
        block = pl.ds(h * half, half)
        kv_copies.append(
            [
                pltpu.make_async_copy(a.at[block], b.at[block], kv_sem.at[i, h])
                for i, (a, b) in enumerate([(q_hbm, q), (k_hbm, kc), (v_hbm, vc)])
            ]
        )
        for c in kv_copies[h]:
            c.start()
    copies = [
        pltpu.make_async_copy(wo_hbm, wo, w_sem.at[0]),
        pltpu.make_async_copy(wg_hbm.at[0], wg.at[0], w_sem.at[1]),
        pltpu.make_async_copy(wg_hbm.at[1], wg.at[1], w_sem.at[2]),
        pltpu.make_async_copy(wd_hbm, wd, w_sem.at[3]),
    ]
    copies[0].start()

    barrier = pltpu.get_barrier_semaphore()
    pl.semaphore_signal(
        barrier, inc=1, device_id={"tp": 1 - t}, device_id_type=pl.DeviceIdType.MESH
    )

    def greet(d):
        pl.semaphore_signal(
            barrier,
            inc=1,
            device_id={"sect": (s + d) % S},
            device_id_type=pl.DeviceIdType.MESH,
        )

    each(S, 1, greet)

    def slot(k, direction):
        if k == 0:
            return 0
        return 2 * k - 1 if direction == 0 or k == ring_half else 2 * k

    def ring_copy(k, direction, h):
        return remote(
            gath.at[pl.ds(slot(k - 1, direction) * rows + h * half, half)],
            gath.at[pl.ds(slot(k, direction) * rows + h * half, half)],
            ring_send.at[direction, k - 1, h],
            ring_recv.at[direction, k - 1, h],
            sect=right if direction == 0 else left,
        )

    def ring_pairs(k):
        return [(0, 0), (1, 1)] if k == ring_half else [(0, 0), (1, 0), (0, 1), (1, 1)]

    positions = lax.broadcasted_iota(jnp.int32, (heads_count, context), 1)
    inverse_root = 1.0 / math.sqrt(head_dim)
    for h in range(2):
        for c in kv_copies[h]:
            c.wait()
        for first in range(h * half, (h + 1) * half, 4):
            group = range(first, first + 4)
            weights = []
            for r in group:
                score = lax.dot_general(
                    q[r], kc[r], (((1,), (1,)), ((), ())), preferred_element_type=f32
                )
                score = jnp.where(positions < lengths[r], score * inverse_root, -1e30)
                exponent = jnp.exp(score - jnp.max(score, axis=1, keepdims=True))
                total = jnp.sum(exponent, axis=1, keepdims=True)
                weights.append((exponent * (1.0 / total)).astype(bf16))
            for r, w in zip(group, weights):
                attn[r * heads_count : (r + 1) * heads_count] = jnp.dot(
                    w, vc[r], preferred_element_type=f32
                )
        for n in range(heads_count):
            gath[h * half : (h + 1) * half, n * head_dim : (n + 1) * head_dim] = attn[
                pl.ds(h * half * heads_count + n, half, stride=heads_count), :
            ].astype(bf16)
        if h == 0:
            pl.semaphore_wait(barrier, S)
        for direction in range(2):
            ring_copy(1, direction, h).start()
    for c in copies[1:]:
        c.start()

    bands = [jnp.zeros((1, rows), jnp.int32) for _ in range(top_count)]
    for k in range(top_count):
        named = chosen[k : k + 1, :]
        for e in range(experts):
            bands[k] = jnp.where(named == e, home[e], bands[k])
    band_ids = lax.broadcasted_iota(jnp.int32, (experts, rows), 0)
    member = jnp.zeros((experts, rows), f32)
    weight = jnp.zeros((experts, rows), f32)
    for k in range(top_count):
        member = jnp.where(band_ids == bands[k], 1.0, member)
        weight = jnp.where(band_ids == bands[k], probs[k : k + 1, :], weight)
    before = (
        lax.broadcasted_iota(jnp.int32, (rows, rows), 0)
        < lax.broadcasted_iota(jnp.int32, (rows, rows), 1)
    ).astype(bf16)
    rank = jnp.dot(member.astype(bf16), before, preferred_element_type=f32)
    rank = jnp.where(member > 0.0, rank, -1.0)
    places = lax.broadcasted_iota(jnp.int32, (cap, rows), 0).astype(f32)
    mix_parts = []
    for d in range(S):
        b = d // band_size
        hit = rank[b : b + 1, :] == places
        selector[d * cap : (d + 1) * cap] = jnp.where(hit, 1.0, 0.0).astype(bf16)
        mix_parts.append(jnp.where(hit, weight[b : b + 1, :], 0.0))
    mixing[...] = jnp.concatenate(mix_parts, axis=0).T

    def exchange(o):
        return remote(
            part.at[o, 1 - t],
            tp_in.at[o],
            tpx_send.at[o],
            tpx_recv.at[o],
            tp=1 - t,
        )

    def rel_of(o):
        if o == 0:
            return 0
        k = (o + 1) // 2
        return -k if o % 2 == 1 else k

    def feature_copy(o):
        return remote(
            feat_out.at[o],
            feat_in.at[s],
            feat_send.at[o],
            feat_recv.at[s],
            sect=owner(rel_of(o)),
        )

    def feature_arrival(j):
        return remote(feat_out.at[0], feat_in.at[j], feat_send.at[0], feat_recv.at[j], sect=j)

    def finish(o):
        exchange(o).wait_recv()
        total = part[o, t] + tp_in[o]
        if o == 0:
            feat_in[s] = total.astype(bf16)
        else:
            feat_out[o] = total.astype(bf16)
            feature_copy(o).start()

    def project(first, count):
        product = lax.dot_general(
            gath[first * rows : (first + count) * rows],
            wo[...],
            (((1,), (1,)), ((), ())),
            preferred_element_type=f32,
        )
        for b in range(count):
            for h in range(2):
                part[first + b, h] = product[b * rows + h * half : b * rows + (h + 1) * half]
            exchange(first + b).start()

    copies[0].wait()
    project(0, 1)
    waiting = [0]
    for k in range(1, ring_half + 1):
        for direction, h in ring_pairs(k):
            ring_copy(k, direction, h).wait_recv()
            if k < ring_half and (direction, h) in ring_pairs(k + 1):
                ring_copy(k + 1, direction, h).start()
        if k < ring_half:
            project(2 * k - 1, 2)
            for o in waiting:
                finish(o)
            waiting = [2 * k - 1, 2 * k]
        else:
            project(S - 1, 1)
            for o in waiting:
                finish(o)
            finish(S - 1)

    my_half = pl.ds(pl.multiple_of(t * half, half), half)
    their_half = pl.ds(pl.multiple_of((1 - t) * half, half), half)

    def await_features(d):
        feature_arrival((s + d) % S).wait_recv()

    each(S, 1, await_features)
    features = jnp.concatenate([feat_in[j].astype(f32) for j in range(S)], axis=1)
    a = resid[my_half, :].astype(f32) + features
    attended[my_half, :] = a
    scale = lax.rsqrt(jnp.sum(a * a, axis=1, keepdims=True) * (1.0 / D) + 1e-06)
    normed[my_half, :] = (a * scale * gain[...]).astype(bf16)
    normed_copy = remote(
        normed.at[my_half], normed.at[my_half], nx_send.at[0], nx_recv.at[0], tp=1 - t
    )
    normed_copy.start()

    def columns(core, c):
        return pl.ds(pl.multiple_of(core * H + starts[c], 128), widths[c])

    my_columns = pl.ds(pl.multiple_of(t * H, 128), H)
    their_columns = pl.ds(pl.multiple_of((1 - t) * H, 128), H)
    att_copy = remote(
        attended.at[my_half, their_columns],
        attended.at[my_half, their_columns],
        nx_send.at[1],
        nx_recv.at[1],
        tp=1 - t,
    )
    att_copy.start()
    remote(
        normed.at[their_half], normed.at[their_half], nx_send.at[0], nx_recv.at[0], tp=1 - t
    ).wait_recv()

    def slots_of(j):
        return pl.ds(pl.multiple_of(j * cap, cap), cap)

    def dispatch_copy(c, d):
        dest = (s + d) % S
        return remote(
            packed.at[slots_of(dest), pl.ds(starts[c], widths[c])],
            xbuf.at[slots_of(s), columns(t, c)],
            disp_send.at[c, d],
            disp_recv.at[c, d],
            sect=dest,
        )

    def dispatch_arrival(c, d):
        sender = (s - d + S) % S
        return remote(
            packed.at[slots_of(sender), pl.ds(starts[c], widths[c])],
            xbuf.at[slots_of(sender), columns(t, c)],
            disp_send.at[c, d],
            disp_recv.at[c, d],
            sect=sender,
        )

    def share_copy(c, core):
        block = xbuf.at[:, columns(core, c)]
        return remote(block, block, share_send.at[c], share_recv.at[c], tp=1 - t)

    for c in range(NC):
        packed[:, starts[c] : starts[c] + widths[c]] = jnp.dot(
            selector[...], normed[:, columns(t, c)], preferred_element_type=f32
        ).astype(bf16)
        each(S, 1, lambda d: dispatch_copy(c, d).start())
        xbuf[slots_of(s), columns(t, c)] = packed[
            slots_of(s), starts[c] : starts[c] + widths[c]
        ]

    copies[1].wait()
    copies[2].wait()

    def accumulate(c, core, first=False):
        x = xbuf[:, columns(core, c)]
        for m in range(2):
            product = jnp.dot(x, wg[m, columns(core, c), :], preferred_element_type=f32)
            if first:
                acc[m] = product
            else:
                acc[m] += product

    for c in range(NC):
        each(S, 1, lambda d: dispatch_arrival(c, d).wait_recv())
        share_copy(c, t).start()
        accumulate(c, t, first=c == 0)
        if c > 0:
            share_copy(c - 1, 1 - t).wait_recv()
            accumulate(c - 1, 1 - t)
    share_copy(NC - 1, 1 - t).wait_recv()
    accumulate(NC - 1, 1 - t)

    gate_value = acc[0]
    act[...] = (gate_value / (1.0 + jnp.exp(-gate_value)) * acc[1]).astype(bf16)
    copies[3].wait()

    def chunk(c):
        return pl.ds(starts[c], widths[c])

    def down_copy(c):
        return remote(
            down_out.at[:, chunk(c)],
            down_in.at[:, chunk(c)],
            dx_send.at[c],
            dx_recv.at[c],
            tp=1 - t,
        )

    def return_copy(c, d):
        dest = (s + d) % S
        return remote(
            ret_out.at[slots_of(dest), chunk(c)],
            ret_in.at[slots_of(s), chunk(c)],
            ret_send.at[c, d],
            ret_recv.at[c, d],
            sect=dest,
        )

    def return_arrival(c, d):
        sender = (s - d + S) % S
        return remote(
            ret_out.at[slots_of(sender), chunk(c)],
            ret_in.at[slots_of(sender), chunk(c)],
            ret_send.at[c, d],
            ret_recv.at[c, d],
            sect=sender,
        )

    for c in range(NC):
        cols = slice(starts[c], starts[c] + widths[c])
        down_out[:, cols] = jnp.dot(
            act[...], wd[:, columns(1 - t, c)], preferred_element_type=f32
        ).astype(bf16)
        down_copy(c).start()
        own = jnp.dot(act[...], wd[:, columns(t, c)], preferred_element_type=f32)
        down_copy(c).wait_recv()
        ret_out[:, cols] = (own.astype(bf16).astype(f32) + down_in[:, cols].astype(f32)).astype(
            bf16
        )
        each(S, 1, lambda d: return_copy(c, d).start())
        ret_in[slots_of(s), cols] = ret_out[slots_of(s), cols]

    mix = mixing[...]
    mix_high = mix.astype(bf16)
    rest = mix - mix_high.astype(f32)
    mix_mid = rest.astype(bf16)
    mix_low = (rest - mix_mid.astype(f32)).astype(bf16)
    remote(
        attended.at[their_half, my_columns],
        attended.at[their_half, my_columns],
        nx_send.at[1],
        nx_recv.at[1],
        tp=1 - t,
    ).wait_recv()
    for c in range(NC):
        cols = slice(starts[c], starts[c] + widths[c])
        each(S, 1, lambda d: return_arrival(c, d).wait_recv())
        got = ret_in[:, cols]
        expert_sum = (
            jnp.dot(mix_high, got, preferred_element_type=f32)
            + jnp.dot(mix_mid, got, preferred_element_type=f32)
            + jnp.dot(mix_low, got, preferred_element_type=f32)
        )
        out[:, cols] = (attended[:, columns(t, c)] + expert_sum).astype(bf16)

    for k in range(1, ring_half + 1):
        for direction, h in ring_pairs(k):
            ring_copy(k, direction, h).wait_send()
    for o in range(S):
        exchange(o).wait_send()
        if o > 0:
            feature_copy(o).wait_send()
    normed_copy.wait_send()
    att_copy.wait_send()
    for c in range(NC):
        each(S, 1, lambda d: dispatch_copy(c, d).wait_send())
        share_copy(c, t).wait_send()
        down_copy(c).wait_send()
        each(S, 1, lambda d: return_copy(c, d).wait_send())


def chunk_widths(total):
    unit = 256 if total % 256 == 0 else 128
    units = total // unit
    base, extra = units // 3, units % 3
    return tuple(unit * (base + (1 if c < extra else 0)) for c in range(3))


def layer_call(S, lengths, home, q, k, v, wo_t, resid, gain, chosen, probs, gate_up, down_proj):
    f32, bf16 = jnp.float32, jnp.bfloat16
    rows, heads_count, head_dim = q.shape
    half = rows // 2
    F = wo_t.shape[0]
    D = F * S
    hidden = down_proj.shape[0]
    slots = S * (rows // CAP_SHARE)
    widths = chunk_widths(D // 2)
    NC = len(widths)
    dma = pltpu.SemaphoreType.DMA
    vmem = pl.BlockSpec(memory_space=pltpu.VMEM)
    smem = pl.BlockSpec(memory_space=pltpu.SMEM)
    hbm = pl.BlockSpec(memory_space=pl.ANY)
    return pl.pallas_call(
        functools.partial(layer_kernel, S, widths),
        out_shape=jax.ShapeDtypeStruct((rows, D // 2), bf16),
        in_specs=[smem, smem, hbm, hbm, hbm, hbm, vmem, vmem, vmem, vmem, hbm, hbm],
        out_specs=vmem,
        scratch_shapes=[
            pltpu.VMEM(q.shape, bf16),
            pltpu.VMEM(k.shape, bf16),
            pltpu.VMEM(v.shape, bf16),
            pltpu.VMEM(wo_t.shape, bf16),
            pltpu.VMEM(gate_up.shape, bf16),
            pltpu.VMEM(down_proj.shape, bf16),
            pltpu.VMEM((rows * heads_count, head_dim), f32),
            pltpu.VMEM((S * rows, heads_count * head_dim), bf16),
            pltpu.VMEM((S, 2, half, F), f32),
            pltpu.VMEM((S, half, F), f32),
            pltpu.VMEM((S, half, F), bf16),
            pltpu.VMEM((S, half, F), bf16),
            pltpu.VMEM((rows, D), bf16),
            pltpu.VMEM((rows, D), f32),
            pltpu.VMEM((slots, rows), bf16),
            pltpu.VMEM((rows, slots), f32),
            pltpu.VMEM((slots, D // 2), bf16),
            pltpu.VMEM((slots, D), bf16),
            pltpu.VMEM((2, slots, hidden), f32),
            pltpu.VMEM((slots, hidden), bf16),
            pltpu.VMEM((slots, D // 2), bf16),
            pltpu.VMEM((slots, D // 2), bf16),
            pltpu.VMEM((slots, D // 2), bf16),
            pltpu.VMEM((slots, D // 2), bf16),
            dma((3, 2)),
            dma((4,)),
            dma((2, S // 2, 2)),
            dma((2, S // 2, 2)),
            dma((S,)),
            dma((S,)),
            dma((S,)),
            dma((S,)),
            dma((2,)),
            dma((2,)),
            dma((NC, S)),
            dma((NC, S)),
            dma((NC,)),
            dma((NC,)),
            dma((NC,)),
            dma((NC,)),
            dma((NC, S)),
            dma((NC, S)),
        ],
        compiler_params=pltpu.CompilerParams(
            collective_id=0, has_side_effects=True, vmem_limit_bytes=58 * 1024 * 1024
        ),
        cost_estimate=pl.CostEstimate(
            flops=2 * S * rows * wo_t.size + 6 * slots * D * hidden,
            bytes_accessed=2 * (wo_t.size + gate_up.size + down_proj.size),
            transcendentals=slots * hidden,
        ),
    )(lengths, home, q, k, v, wo_t, resid, gain, chosen, probs, gate_up, down_proj)


def body(
    queries,
    keys,
    values,
    kv_lengths,
    out_proj,
    resid,
    norm_gain,
    experts_chosen,
    route_probs,
    expert_home,
    gate_up,
    down_proj,
):
    row_count, context, _, head_dim = keys.shape
    return layer_call(
        lax.axis_size("sect"),
        kv_lengths,
        expert_home,
        queries,
        keys.reshape(row_count, context, head_dim),
        values.reshape(row_count, context, head_dim),
        out_proj.T,
        resid,
        norm_gain.astype(jnp.float32).reshape(1, -1),
        experts_chosen.T,
        route_probs.T,
        gate_up,
        down_proj,
    )


def solution(mesh):
    in_specs = (
        P(("groups", "sect"), "tp", None),
        P(("groups", "sect"), None, "tp", None),
        P(("groups", "sect"), None, "tp", None),
        P(("groups", "sect")),
        P("tp", "sect"),
        P(("groups", "sect"), None),
        P(),
        P(("groups", "sect"), None),
        P(("groups", "sect"), None),
        P(),
        P(None, None, ("sect", "tp")),
        P(("sect", "tp"), None),
    )
    out_specs = P(("groups", "sect"), "tp")
    return jax.shard_map(body, mesh=mesh, in_specs=in_specs, out_specs=out_specs, check_vma=False)
```

```python
import functools
import math

import jax
import jax.numpy as jnp
from jax import lax
from jax.experimental import pallas as pl
from jax.experimental.pallas import tpu as pltpu
from jax.sharding import PartitionSpec as P

CAP_SHARE = 2


def each(count, start, f):
    if count <= 8:
        for i in sorted(range(start, count), key=lambda i: -min(i, count - i)):
            f(i)
    else:

        def step(i, carry):
            f(i)
            return carry

        lax.fori_loop(start, count, step, 0)


def layer_kernel(
    S,
    widths,
    lengths,
    home,
    q_hbm,
    k_hbm,
    v_hbm,
    wo_hbm,
    resid,
    gain,
    chosen,
    probs,
    wg_hbm,
    wd_hbm,
    out,
    q,
    kc,
    vc,
    wo,
    wg,
    wd,
    attn,
    gath,
    part,
    tp_in,
    feat_out,
    feat_in,
    normed,
    attended,
    selector,
    mixing,
    packed,
    xbuf,
    acc,
    act,
    down_out,
    down_in,
    ret_out,
    ret_in,
    kv_sem,
    w_sem,
    ring_send,
    ring_recv,
    tpx_send,
    tpx_recv,
    feat_send,
    feat_recv,
    nx_send,
    nx_recv,
    disp_send,
    disp_recv,
    share_send,
    share_recv,
    dx_send,
    dx_recv,
    ret_send,
    ret_recv,
):
    f32, bf16 = jnp.float32, jnp.bfloat16
    s = lax.axis_index("sect")
    t = lax.axis_index("tp")
    rows, heads_count, head_dim = q.shape
    context = kc.shape[1]
    half = rows // 2
    F = wo.shape[0]
    D = F * S
    H = D // 2
    cap = xbuf.shape[0] // S
    experts = home.shape[0]
    band_size = S // experts
    top_count = chosen.shape[0]
    NC = len(widths)
    starts = [sum(widths[:c]) for c in range(NC)]
    back, back_starts = widths[::-1], starts[::-1]
    ring_half = S // 2
    K_half = heads_count * head_dim // 2

    def ring_index(p):
        return jnp.where(p < ring_half, 2 * p, 2 * (S - 1 - p) + 1)

    pos = jnp.where(s % 2 == 0, s // 2, S - 1 - (s - 1) // 2)

    def owner(rel):
        return ring_index((pos + rel + S) % S)

    right, left = owner(1), owner(-1)

    def remote(src, dst, ss, rs, **dev):
        return pltpu.make_async_remote_copy(
            src_ref=src,
            dst_ref=dst,
            send_sem=ss,
            recv_sem=rs,
            device_id=dev,
            device_id_type=pl.DeviceIdType.MESH,
        )

    kv_copies = []
    for h in range(2):
        block = pl.ds(h * half, half)
        kv_copies.append(
            [
                pltpu.make_async_copy(a.at[block], b.at[block], kv_sem.at[i, h])
                for i, (a, b) in enumerate([(q_hbm, q), (k_hbm, kc), (v_hbm, vc)])
            ]
        )
        for c in kv_copies[h]:
            c.start()
    copies = [
        pltpu.make_async_copy(wo_hbm, wo, w_sem.at[0]),
        pltpu.make_async_copy(wg_hbm.at[0], wg.at[0], w_sem.at[1]),
        pltpu.make_async_copy(wg_hbm.at[1], wg.at[1], w_sem.at[2]),
        pltpu.make_async_copy(wd_hbm, wd, w_sem.at[3]),
    ]
    copies[0].start()

    barrier = pltpu.get_barrier_semaphore()
    pl.semaphore_signal(
        barrier, inc=1, device_id={"tp": 1 - t}, device_id_type=pl.DeviceIdType.MESH
    )

    def greet(d):
        pl.semaphore_signal(
            barrier,
            inc=1,
            device_id={"sect": (s + d) % S},
            device_id_type=pl.DeviceIdType.MESH,
        )

    each(S, 1, greet)

    def slot(k, direction):
        if k == 0:
            return 0
        return 2 * k - 1 if direction == 0 or k == ring_half else 2 * k

    def ring_copy(k, direction, h):
        if k == ring_half:
            cols = pl.ds(h * K_half, K_half)
            return remote(
                gath.at[pl.ds(slot(k - 1, direction) * rows + direction * half, half), cols],
                gath.at[pl.ds(slot(k, direction) * rows + direction * half, half), cols],
                ring_send.at[direction, k - 1, h],
                ring_recv.at[direction, k - 1, h],
                sect=right if direction == 0 else left,
            )
        return remote(
            gath.at[pl.ds(slot(k - 1, direction) * rows + h * half, half)],
            gath.at[pl.ds(slot(k, direction) * rows + h * half, half)],
            ring_send.at[direction, k - 1, h],
            ring_recv.at[direction, k - 1, h],
            sect=right if direction == 0 else left,
        )

    ring_pairs = [(0, 0), (1, 0), (0, 1), (1, 1)]

    positions = lax.broadcasted_iota(jnp.int32, (heads_count, context), 1)
    inverse_root = 1.0 / math.sqrt(head_dim)
    for h in range(2):
        for c in kv_copies[h]:
            c.wait()
        for first in range(h * half, (h + 1) * half, 4):
            group = range(first, first + 4)
            weights = []
            for r in group:
                score = lax.dot_general(
                    q[r], kc[r], (((1,), (1,)), ((), ())), preferred_element_type=f32
                )
                score = jnp.where(positions < lengths[r], score * inverse_root, -1e30)
                exponent = jnp.exp(score - jnp.max(score, axis=1, keepdims=True))
                total = jnp.sum(exponent, axis=1, keepdims=True)
                weights.append((exponent * (1.0 / total)).astype(bf16))
            for r, w in zip(group, weights):
                attn[r * heads_count : (r + 1) * heads_count] = jnp.dot(
                    w, vc[r], preferred_element_type=f32
                )
        for n in range(heads_count):
            gath[h * half : (h + 1) * half, n * head_dim : (n + 1) * head_dim] = attn[
                pl.ds(h * half * heads_count + n, half, stride=heads_count), :
            ].astype(bf16)
        if h == 0:
            pl.semaphore_wait(barrier, S)
        for direction in range(2):
            ring_copy(1, direction, h).start()
    for c in copies[1:]:
        c.start()

    bands = [jnp.zeros((1, rows), jnp.int32) for _ in range(top_count)]
    for k in range(top_count):
        named = chosen[k : k + 1, :]
        for e in range(experts):
            bands[k] = jnp.where(named == e, home[e], bands[k])
    band_ids = lax.broadcasted_iota(jnp.int32, (experts, rows), 0)
    member = jnp.zeros((experts, rows), f32)
    weight = jnp.zeros((experts, rows), f32)
    for k in range(top_count):
        member = jnp.where(band_ids == bands[k], 1.0, member)
        weight = jnp.where(band_ids == bands[k], probs[k : k + 1, :], weight)
    before = (
        lax.broadcasted_iota(jnp.int32, (rows, rows), 0)
        < lax.broadcasted_iota(jnp.int32, (rows, rows), 1)
    ).astype(bf16)
    rank = jnp.dot(member.astype(bf16), before, preferred_element_type=f32)
    rank = jnp.where(member > 0.0, rank, -1.0)
    places = lax.broadcasted_iota(jnp.int32, (cap, rows), 0).astype(f32)
    mix_parts = []
    for d in range(S):
        b = d // band_size
        hit = rank[b : b + 1, :] == places
        selector[d * cap : (d + 1) * cap] = jnp.where(hit, 1.0, 0.0).astype(bf16)
        mix_parts.append(jnp.where(hit, weight[b : b + 1, :], 0.0))
    mixing[...] = jnp.concatenate(mix_parts, axis=0).T

    def exchange(o):
        return remote(
            part.at[o, 1 - t],
            tp_in.at[o],
            tpx_send.at[o],
            tpx_recv.at[o],
            tp=1 - t,
        )

    def rel_of(o):
        if o == 0:
            return 0
        k = (o + 1) // 2
        return -k if o % 2 == 1 else k

    def feature_copy(o):
        return remote(
            feat_out.at[o],
            feat_in.at[s],
            feat_send.at[o],
            feat_recv.at[s],
            sect=owner(rel_of(o)),
        )

    def feature_arrival(j):
        return remote(feat_out.at[0], feat_in.at[j], feat_send.at[0], feat_recv.at[j], sect=j)

    def finish(o):
        exchange(o).wait_recv()
        total = part[o, t] + tp_in[o]
        if o == 0:
            feat_in[s] = total.astype(bf16)
        else:
            feat_out[o] = total.astype(bf16)
            feature_copy(o).start()

    def product_of(first, count, cols):
        return lax.dot_general(
            gath[first * rows : (first + count) * rows, cols],
            wo[:, cols],
            (((1,), (1,)), ((), ())),
            preferred_element_type=f32,
        )

    def project(first, count, product):
        for b in range(count):
            for h in range(2):
                part[first + b, h] = product[b * rows + h * half : b * rows + (h + 1) * half]
            exchange(first + b).start()

    copies[0].wait()
    project(0, 1, product_of(0, 1, slice(None)))
    waiting = [0]
    for k in range(1, ring_half):
        for direction, h in ring_pairs:
            ring_copy(k, direction, h).wait_recv()
            if k + 1 < ring_half:
                ring_copy(k + 1, direction, h).start()
            elif direction == h:
                ring_copy(k + 1, direction, 0).start()
                ring_copy(k + 1, direction, 1).start()
            if (direction, h) == (1, 0):
                for o in waiting:
                    finish(o)
        project(2 * k - 1, 2, product_of(2 * k - 1, 2, slice(None)))
        waiting = [2 * k - 1, 2 * k]
    for o in waiting:
        finish(o)
    product = None
    for h in range(2):
        for direction in range(2):
            ring_copy(ring_half, direction, h).wait_recv()
        more = product_of(S - 1, 1, slice(h * K_half, (h + 1) * K_half))
        product = more if product is None else product + more
    project(S - 1, 1, product)
    finish(S - 1)

    my_half = pl.ds(pl.multiple_of(t * half, half), half)
    their_half = pl.ds(pl.multiple_of((1 - t) * half, half), half)

    def await_features(d):
        feature_arrival((s + d) % S).wait_recv()

    each(S, 1, await_features)
    features = jnp.concatenate([feat_in[j].astype(f32) for j in range(S)], axis=1)
    a = resid[my_half, :].astype(f32) + features
    attended[my_half, :] = a
    scale = lax.rsqrt(jnp.sum(a * a, axis=1, keepdims=True) * (1.0 / D) + 1e-06)
    normed[my_half, :] = (a * scale * gain[...].astype(f32).reshape(1, D)).astype(bf16)
    normed_copy = remote(
        normed.at[my_half], normed.at[my_half], nx_send.at[0], nx_recv.at[0], tp=1 - t
    )
    normed_copy.start()

    def columns(core, c):
        return pl.ds(pl.multiple_of(core * H + starts[c], 128), widths[c])

    my_columns = pl.ds(pl.multiple_of(t * H, 128), H)
    their_columns = pl.ds(pl.multiple_of((1 - t) * H, 128), H)
    att_copy = remote(
        attended.at[my_half, their_columns],
        attended.at[my_half, their_columns],
        nx_send.at[1],
        nx_recv.at[1],
        tp=1 - t,
    )
    att_copy.start()
    remote(
        normed.at[their_half], normed.at[their_half], nx_send.at[0], nx_recv.at[0], tp=1 - t
    ).wait_recv()

    def slots_of(j):
        return pl.ds(pl.multiple_of(j * cap, cap), cap)

    def dispatch_copy(c, d):
        dest = (s + d) % S
        return remote(
            packed.at[slots_of(dest), pl.ds(starts[c], widths[c])],
            xbuf.at[slots_of(s), columns(t, c)],
            disp_send.at[c, d],
            disp_recv.at[c, d],
            sect=dest,
        )

    def dispatch_arrival(c, d):
        sender = (s - d + S) % S
        return remote(
            packed.at[slots_of(sender), pl.ds(starts[c], widths[c])],
            xbuf.at[slots_of(sender), columns(t, c)],
            disp_send.at[c, d],
            disp_recv.at[c, d],
            sect=sender,
        )

    def share_copy(c, core):
        block = xbuf.at[:, columns(core, c)]
        return remote(block, block, share_send.at[c], share_recv.at[c], tp=1 - t)

    for c in range(NC):
        packed[:, starts[c] : starts[c] + widths[c]] = jnp.dot(
            selector[...], normed[:, columns(t, c)], preferred_element_type=f32
        ).astype(bf16)
        each(S, 1, lambda d: dispatch_copy(c, d).start())
        xbuf[slots_of(s), columns(t, c)] = packed[
            slots_of(s), starts[c] : starts[c] + widths[c]
        ]

    copies[1].wait()
    copies[2].wait()

    def accumulate(c, core, first=False):
        x = xbuf[:, columns(core, c)]
        for m in range(2):
            product = jnp.dot(x, wg[m, columns(core, c), :], preferred_element_type=f32)
            if first:
                acc[m] = product
            else:
                acc[m] += product

    for c in range(NC):
        each(S, 1, lambda d: dispatch_arrival(c, d).wait_recv())
        share_copy(c, t).start()
        accumulate(c, t, first=c == 0)
        if c > 0:
            share_copy(c - 1, 1 - t).wait_recv()
            accumulate(c - 1, 1 - t)
    share_copy(NC - 1, 1 - t).wait_recv()
    accumulate(NC - 1, 1 - t)

    gate_value = acc[0]
    act[...] = (gate_value / (1.0 + jnp.exp(-gate_value)) * acc[1]).astype(bf16)
    copies[3].wait()

    def chunk(c):
        return pl.ds(back_starts[c], back[c])

    def down_copy(c):
        return remote(
            down_out.at[:, chunk(c)],
            down_in.at[:, chunk(c)],
            dx_send.at[c],
            dx_recv.at[c],
            tp=1 - t,
        )

    def return_copy(c, d):
        dest = (s + d) % S
        return remote(
            ret_out.at[slots_of(dest), chunk(c)],
            ret_in.at[slots_of(s), chunk(c)],
            ret_send.at[c, d],
            ret_recv.at[c, d],
            sect=dest,
        )

    def return_arrival(c, d):
        sender = (s - d + S) % S
        return remote(
            ret_out.at[slots_of(sender), chunk(c)],
            ret_in.at[slots_of(sender), chunk(c)],
            ret_send.at[c, d],
            ret_recv.at[c, d],
            sect=sender,
        )

    for c in range(NC):
        cols = slice(back_starts[c], back_starts[c] + back[c])
        down_out[:, cols] = jnp.dot(
            act[...], wd[:, columns(1 - t, NC - 1 - c)], preferred_element_type=f32
        ).astype(bf16)
        down_copy(c).start()
        own = jnp.dot(act[...], wd[:, columns(t, NC - 1 - c)], preferred_element_type=f32)
        down_copy(c).wait_recv()
        ret_out[:, cols] = (own.astype(bf16).astype(f32) + down_in[:, cols].astype(f32)).astype(
            bf16
        )
        each(S, 1, lambda d: return_copy(c, d).start())
        ret_in[slots_of(s), cols] = ret_out[slots_of(s), cols]

    mix = mixing[...]
    mix_high = mix.astype(bf16)
    rest = mix - mix_high.astype(f32)
    mix_mid = rest.astype(bf16)
    mix_low = (rest - mix_mid.astype(f32)).astype(bf16)
    remote(
        attended.at[their_half, my_columns],
        attended.at[their_half, my_columns],
        nx_send.at[1],
        nx_recv.at[1],
        tp=1 - t,
    ).wait_recv()
    for c in range(NC):
        cols = slice(back_starts[c], back_starts[c] + back[c])
        each(S, 1, lambda d: return_arrival(c, d).wait_recv())
        got = ret_in[:, cols]
        expert_sum = (
            jnp.dot(mix_high, got, preferred_element_type=f32)
            + jnp.dot(mix_mid, got, preferred_element_type=f32)
            + jnp.dot(mix_low, got, preferred_element_type=f32)
        )
        out[:, cols] = (attended[:, columns(t, NC - 1 - c)] + expert_sum).astype(bf16)

    for k in range(1, ring_half + 1):
        for direction, h in ring_pairs:
            ring_copy(k, direction, h).wait_send()
    for o in range(S):
        exchange(o).wait_send()
        if o > 0:
            feature_copy(o).wait_send()
    normed_copy.wait_send()
    att_copy.wait_send()
    for c in range(NC):
        each(S, 1, lambda d: dispatch_copy(c, d).wait_send())
        share_copy(c, t).wait_send()
        down_copy(c).wait_send()
        each(S, 1, lambda d: return_copy(c, d).wait_send())


def chunk_widths(total):
    unit = 256 if total % 256 == 0 else 128
    units = total // unit
    widths = [2 * unit] * (units // 2)
    return tuple(widths + [unit] * (units % 2))


def layer_call(S, lengths, home, q, k, v, wo_t, resid, gain, chosen, probs, gate_up, down_proj):
    f32, bf16 = jnp.float32, jnp.bfloat16
    rows, heads_count, head_dim = q.shape
    half = rows // 2
    F = wo_t.shape[0]
    D = F * S
    hidden = down_proj.shape[0]
    slots = S * (rows // CAP_SHARE)
    widths = chunk_widths(D // 2)
    NC = len(widths)
    dma = pltpu.SemaphoreType.DMA
    vmem = pl.BlockSpec(memory_space=pltpu.VMEM)
    smem = pl.BlockSpec(memory_space=pltpu.SMEM)
    hbm = pl.BlockSpec(memory_space=pl.ANY)
    return pl.pallas_call(
        functools.partial(layer_kernel, S, widths),
        out_shape=pltpu.VMEM((rows, D // 2), bf16),
        in_specs=[smem, smem, hbm, hbm, hbm, hbm, vmem, vmem, vmem, vmem, hbm, hbm],
        out_specs=vmem,
        scratch_shapes=[
            pltpu.VMEM(q.shape, bf16),
            pltpu.VMEM(k.shape, bf16),
            pltpu.VMEM(v.shape, bf16),
            pltpu.VMEM(wo_t.shape, bf16),
            pltpu.VMEM(gate_up.shape, bf16),
            pltpu.VMEM(down_proj.shape, bf16),
            pltpu.VMEM((rows * heads_count, head_dim), f32),
            pltpu.VMEM((S * rows, heads_count * head_dim), bf16),
            pltpu.VMEM((S, 2, half, F), f32),
            pltpu.VMEM((S, half, F), f32),
            pltpu.VMEM((S, half, F), bf16),
            pltpu.VMEM((S, half, F), bf16),
            pltpu.VMEM((rows, D), bf16),
            pltpu.VMEM((rows, D), f32),
            pltpu.VMEM((slots, rows), bf16),
            pltpu.VMEM((rows, slots), f32),
            pltpu.VMEM((slots, D // 2), bf16),
            pltpu.VMEM((slots, D), bf16),
            pltpu.VMEM((2, slots, hidden), f32),
            pltpu.VMEM((slots, hidden), bf16),
            pltpu.VMEM((slots, D // 2), bf16),
            pltpu.VMEM((slots, D // 2), bf16),
            pltpu.VMEM((slots, D // 2), bf16),
            pltpu.VMEM((slots, D // 2), bf16),
            dma((3, 2)),
            dma((4,)),
            dma((2, S // 2, 2)),
            dma((2, S // 2, 2)),
            dma((S,)),
            dma((S,)),
            dma((S,)),
            dma((S,)),
            dma((2,)),
            dma((2,)),
            dma((NC, S)),
            dma((NC, S)),
            dma((NC,)),
            dma((NC,)),
            dma((NC,)),
            dma((NC,)),
            dma((NC, S)),
            dma((NC, S)),
        ],
        compiler_params=pltpu.CompilerParams(
            collective_id=0, has_side_effects=True, vmem_limit_bytes=60 * 1024 * 1024
        ),
        cost_estimate=pl.CostEstimate(
            flops=2 * S * rows * wo_t.size + 6 * slots * D * hidden,
            bytes_accessed=2 * (wo_t.size + gate_up.size + down_proj.size),
            transcendentals=slots * hidden,
        ),
    )(lengths, home, q, k, v, wo_t, resid, gain, chosen, probs, gate_up, down_proj)


def body(
    queries,
    keys,
    values,
    kv_lengths,
    out_proj,
    resid,
    norm_gain,
    experts_chosen,
    route_probs,
    expert_home,
    gate_up,
    down_proj,
):
    row_count, context, _, head_dim = keys.shape
    return layer_call(
        lax.axis_size("sect"),
        kv_lengths,
        expert_home,
        queries,
        keys.reshape(row_count, context, head_dim),
        values.reshape(row_count, context, head_dim),
        out_proj.T,
        resid,
        norm_gain,
        experts_chosen.T,
        route_probs.T,
        gate_up,
        down_proj,
    )


def solution(mesh):
    in_specs = (
        P(("groups", "sect"), "tp", None),
        P(("groups", "sect"), None, "tp", None),
        P(("groups", "sect"), None, "tp", None),
        P(("groups", "sect")),
        P("tp", "sect"),
        P(("groups", "sect"), None),
        P(),
        P(("groups", "sect"), None),
        P(("groups", "sect"), None),
        P(),
        P(None, None, ("sect", "tp")),
        P(("sect", "tp"), None),
    )
    out_specs = P(("groups", "sect"), "tp")
    return jax.shard_map(body, mesh=mesh, in_specs=in_specs, out_specs=out_specs, check_vma=False)
```

```python
import functools
import math

import jax
import jax.numpy as jnp
from jax import lax
from jax.experimental import pallas as pl
from jax.experimental.pallas import tpu as pltpu
from jax.sharding import PartitionSpec as P

CAP_SHARE = 2


def each(count, start, f):
    if count <= 8:
        for i in sorted(range(start, count), key=lambda i: -min(i, count - i)):
            f(i)
    else:

        def step(i, carry):
            f(i)
            return carry

        lax.fori_loop(start, count, step, 0)


def each_partner(S, batch, f):
    if S <= 8:
        for d in sorted(range(2 - batch, S, 2), key=lambda d: -min(d, S - d)):
            f(d)
    else:

        def step(i, carry):
            f(2 * i + batch)
            return carry

        lax.fori_loop(1 - batch, S // 2, step, 0)


def layer_kernel(
    S,
    widths,
    lengths,
    home,
    q_hbm,
    k_hbm,
    v_hbm,
    wo_hbm,
    resid,
    gain,
    chosen,
    probs,
    wg_hbm,
    wd_hbm,
    out,
    q,
    kc,
    vc,
    wo,
    wg,
    wd,
    attn,
    gath,
    part,
    tp_in,
    feat_out,
    feat_in,
    normed,
    attended,
    selector,
    mixing,
    packed,
    xbuf,
    acc,
    act,
    down_out,
    down_in,
    ret_out,
    ret_in,
    kv_sem,
    w_sem,
    ring_send,
    ring_recv,
    tpx_send,
    tpx_recv,
    feat_send,
    feat_recv,
    nx_send,
    nx_recv,
    disp_send,
    disp_recv,
    share_send,
    share_recv,
    dx_send,
    dx_recv,
    ret_send,
    ret_recv,
):
    f32, bf16 = jnp.float32, jnp.bfloat16
    s = lax.axis_index("sect")
    t = lax.axis_index("tp")
    rows, heads_count, head_dim = q.shape
    context = kc.shape[1]
    half = rows // 2
    F = wo.shape[0]
    D = F * S
    H = D // 2
    cap = packed.shape[0] // S
    experts = home.shape[0]
    band_size = S // experts
    top_count = chosen.shape[0]
    NC = len(widths)
    starts = [sum(widths[:c]) for c in range(NC)]
    back, back_starts = widths[::-1], starts[::-1]
    ring_half = S // 2
    K_half = heads_count * head_dim // 2

    def ring_index(p):
        return jnp.where(p < ring_half, 2 * p, 2 * (S - 1 - p) + 1)

    pos = jnp.where(s % 2 == 0, s // 2, S - 1 - (s - 1) // 2)

    def owner(rel):
        return ring_index((pos + rel + S) % S)

    right, left = owner(1), owner(-1)

    def remote(src, dst, ss, rs, **dev):
        return pltpu.make_async_remote_copy(
            src_ref=src,
            dst_ref=dst,
            send_sem=ss,
            recv_sem=rs,
            device_id=dev,
            device_id_type=pl.DeviceIdType.MESH,
        )

    kv_copies = []
    for h in range(2):
        block = pl.ds(h * half, half)
        kv_copies.append(
            [
                pltpu.make_async_copy(a.at[block], b.at[block], kv_sem.at[i, h])
                for i, (a, b) in enumerate([(q_hbm, q), (k_hbm, kc), (v_hbm, vc)])
            ]
        )
        for c in kv_copies[h]:
            c.start()
    copies = [
        pltpu.make_async_copy(wo_hbm, wo, w_sem.at[0]),
        pltpu.make_async_copy(wg_hbm.at[0], wg.at[0], w_sem.at[1]),
        pltpu.make_async_copy(wg_hbm.at[1], wg.at[1], w_sem.at[2]),
        pltpu.make_async_copy(wd_hbm, wd, w_sem.at[3]),
    ]
    copies[0].start()

    barrier = pltpu.get_barrier_semaphore()
    pl.semaphore_signal(
        barrier, inc=1, device_id={"tp": 1 - t}, device_id_type=pl.DeviceIdType.MESH
    )

    def greet(d):
        pl.semaphore_signal(
            barrier,
            inc=1,
            device_id={"sect": (s + d) % S},
            device_id_type=pl.DeviceIdType.MESH,
        )

    each(S, 1, greet)

    def slot(k, direction):
        if k == 0:
            return 0
        return 2 * k - 1 if direction == 0 or k == ring_half else 2 * k

    def ring_copy(k, direction, h):
        if k == ring_half:
            cols = pl.ds(h * K_half, K_half)
            return remote(
                gath.at[pl.ds(slot(k - 1, direction) * rows + direction * half, half), cols],
                gath.at[pl.ds(slot(k, direction) * rows + direction * half, half), cols],
                ring_send.at[direction, k - 1, h],
                ring_recv.at[direction, k - 1, h],
                sect=right if direction == 0 else left,
            )
        return remote(
            gath.at[pl.ds(slot(k - 1, direction) * rows + h * half, half)],
            gath.at[pl.ds(slot(k, direction) * rows + h * half, half)],
            ring_send.at[direction, k - 1, h],
            ring_recv.at[direction, k - 1, h],
            sect=right if direction == 0 else left,
        )

    ring_pairs = [(0, 0), (1, 0), (0, 1), (1, 1)]

    positions = lax.broadcasted_iota(jnp.int32, (heads_count, context), 1)
    inverse_root = 1.0 / math.sqrt(head_dim)
    for h in range(2):
        for c in kv_copies[h]:
            c.wait()
        for first in range(h * half, (h + 1) * half, 4):
            group = range(first, first + 4)
            weights = []
            for r in group:
                score = lax.dot_general(
                    q[r], kc[r], (((1,), (1,)), ((), ())), preferred_element_type=f32
                )
                score = jnp.where(positions < lengths[r], score * inverse_root, -1e30)
                exponent = jnp.exp(score - jnp.max(score, axis=1, keepdims=True))
                total = jnp.sum(exponent, axis=1, keepdims=True)
                weights.append((exponent * (1.0 / total)).astype(bf16))
            for r, w in zip(group, weights):
                attn[r * heads_count : (r + 1) * heads_count] = jnp.dot(
                    w, vc[r], preferred_element_type=f32
                )
        for n in range(heads_count):
            gath[h * half : (h + 1) * half, n * head_dim : (n + 1) * head_dim] = attn[
                pl.ds(h * half * heads_count + n, half, stride=heads_count), :
            ].astype(bf16)
        if h == 0:
            pl.semaphore_wait(barrier, S)
        for direction in range(2):
            ring_copy(1, direction, h).start()
    for c in copies[1:]:
        c.start()

    bands = [jnp.zeros((1, rows), jnp.int32) for _ in range(top_count)]
    for k in range(top_count):
        named = chosen[k : k + 1, :]
        for e in range(experts):
            bands[k] = jnp.where(named == e, home[e], bands[k])
    band_ids = lax.broadcasted_iota(jnp.int32, (experts, rows), 0)
    member = jnp.zeros((experts, rows), f32)
    weight = jnp.zeros((experts, rows), f32)
    for k in range(top_count):
        member = jnp.where(band_ids == bands[k], 1.0, member)
        weight = jnp.where(band_ids == bands[k], probs[k : k + 1, :], weight)
    before = (
        lax.broadcasted_iota(jnp.int32, (rows, rows), 0)
        < lax.broadcasted_iota(jnp.int32, (rows, rows), 1)
    ).astype(bf16)
    rank = jnp.dot(member.astype(bf16), before, preferred_element_type=f32)
    rank = jnp.where(member > 0.0, rank, -1.0)
    places = lax.broadcasted_iota(jnp.int32, (cap, rows), 0).astype(f32)
    mix_parts = []
    for d in range(S):
        b = d // band_size
        hit = rank[b : b + 1, :] == places
        selector[d * cap : (d + 1) * cap] = jnp.where(hit, 1.0, 0.0).astype(bf16)
        mix_parts.append(jnp.where(hit, weight[b : b + 1, :], 0.0))
    for parity in range(2):
        mixing[parity] = jnp.concatenate(mix_parts[parity::2], axis=0).T

    def exchange(o):
        return remote(
            part.at[o, 1 - t],
            tp_in.at[o],
            tpx_send.at[o],
            tpx_recv.at[o],
            tp=1 - t,
        )

    def rel_of(o):
        if o == 0:
            return 0
        k = (o + 1) // 2
        return -k if o % 2 == 1 else k

    def feature_copy(o):
        return remote(
            feat_out.at[o],
            feat_in.at[s],
            feat_send.at[o],
            feat_recv.at[s],
            sect=owner(rel_of(o)),
        )

    def feature_arrival(j):
        return remote(feat_out.at[0], feat_in.at[j], feat_send.at[0], feat_recv.at[j], sect=j)

    def finish(o):
        exchange(o).wait_recv()
        total = part[o, t] + tp_in[o]
        if o == 0:
            feat_in[s] = total.astype(bf16)
        else:
            feat_out[o] = total.astype(bf16)
            feature_copy(o).start()

    def product_of(first, count, cols):
        return lax.dot_general(
            gath[first * rows : (first + count) * rows, cols],
            wo[:, cols],
            (((1,), (1,)), ((), ())),
            preferred_element_type=f32,
        )

    def project(first, count, product):
        for b in range(count):
            for h in range(2):
                part[first + b, h] = product[b * rows + h * half : b * rows + (h + 1) * half]
            exchange(first + b).start()

    copies[0].wait()
    project(0, 1, product_of(0, 1, slice(None)))
    waiting = [0]
    for k in range(1, ring_half):
        for direction, h in ring_pairs:
            ring_copy(k, direction, h).wait_recv()
            if k + 1 < ring_half:
                ring_copy(k + 1, direction, h).start()
            elif direction == h:
                ring_copy(k + 1, direction, 0).start()
                ring_copy(k + 1, direction, 1).start()
            if (direction, h) == (1, 0):
                for o in waiting:
                    finish(o)
        project(2 * k - 1, 2, product_of(2 * k - 1, 2, slice(None)))
        waiting = [2 * k - 1, 2 * k]
    for o in waiting:
        finish(o)
    product = None
    for h in range(2):
        for direction in range(2):
            ring_copy(ring_half, direction, h).wait_recv()
        more = product_of(S - 1, 1, slice(h * K_half, (h + 1) * K_half))
        product = more if product is None else product + more
    project(S - 1, 1, product)
    finish(S - 1)

    my_half = pl.ds(pl.multiple_of(t * half, half), half)
    their_half = pl.ds(pl.multiple_of((1 - t) * half, half), half)

    def await_features(d):
        feature_arrival((s + d) % S).wait_recv()

    each(S, 1, await_features)
    features = jnp.concatenate([feat_in[j].astype(f32) for j in range(S)], axis=1)
    a = resid[my_half, :].astype(f32) + features
    attended[my_half, :] = a
    scale = lax.rsqrt(jnp.sum(a * a, axis=1, keepdims=True) * (1.0 / D) + 1e-06)
    normed[my_half, :] = (a * scale * gain[...].astype(f32).reshape(1, D)).astype(bf16)
    normed_copy = remote(
        normed.at[my_half], normed.at[my_half], nx_send.at[0], nx_recv.at[0], tp=1 - t
    )
    normed_copy.start()

    def columns(core, c):
        return pl.ds(pl.multiple_of(core * H + starts[c], 128), widths[c])

    my_columns = pl.ds(pl.multiple_of(t * H, 128), H)
    their_columns = pl.ds(pl.multiple_of((1 - t) * H, 128), H)
    att_copy = remote(
        attended.at[my_half, their_columns],
        attended.at[my_half, their_columns],
        nx_send.at[1],
        nx_recv.at[1],
        tp=1 - t,
    )
    att_copy.start()
    remote(
        normed.at[their_half], normed.at[their_half], nx_send.at[0], nx_recv.at[0], tp=1 - t
    ).wait_recv()

    def slots_of(j):
        return pl.ds(pl.multiple_of(j * cap, cap), cap)

    def pair_slots(j):
        return slots_of(j // 2)

    def dispatch_copy(c, d, batch):
        dest = (s + d) % S
        return remote(
            packed.at[slots_of(dest), pl.ds(starts[c], widths[c])],
            xbuf.at[batch, pair_slots(s), columns(t, c)],
            disp_send.at[c, d],
            disp_recv.at[c, d],
            sect=dest,
        )

    def dispatch_arrival(c, d, batch):
        sender = (s - d + S) % S
        return remote(
            packed.at[slots_of(sender), pl.ds(starts[c], widths[c])],
            xbuf.at[batch, pair_slots(sender), columns(t, c)],
            disp_send.at[c, d],
            disp_recv.at[c, d],
            sect=sender,
        )

    def share_copy(c, core, batch):
        block = xbuf.at[batch, :, columns(core, c)]
        return remote(block, block, share_send.at[batch, c], share_recv.at[batch, c], tp=1 - t)

    for c in range(NC):
        packed[:, starts[c] : starts[c] + widths[c]] = jnp.dot(
            selector[...], normed[:, columns(t, c)], preferred_element_type=f32
        ).astype(bf16)
        each_partner(S, 0, lambda d: dispatch_copy(c, d, 0).start())
        xbuf[0, pair_slots(s), columns(t, c)] = packed[
            slots_of(s), starts[c] : starts[c] + widths[c]
        ]
    for c in range(NC):
        each_partner(S, 1, lambda d: dispatch_copy(c, d, 1).start())

    copies[1].wait()
    copies[2].wait()

    def accumulate(c, core, batch, first=False):
        x = xbuf[batch, :, columns(core, c)]
        for m in range(2):
            product = jnp.dot(x, wg[m, columns(core, c), :], preferred_element_type=f32)
            if first:
                acc[m] = product
            else:
                acc[m] += product

    def chunk(c):
        return pl.ds(back_starts[c], back[c])

    def down_copy(c, batch):
        return remote(
            down_out.at[batch, :, chunk(c)],
            down_in.at[batch, :, chunk(c)],
            dx_send.at[batch, c],
            dx_recv.at[batch, c],
            tp=1 - t,
        )

    def return_copy(c, d, batch):
        dest = (s + d) % S
        return remote(
            ret_out.at[batch, pair_slots(dest), chunk(c)],
            ret_in.at[batch, pair_slots(s), chunk(c)],
            ret_send.at[c, d],
            ret_recv.at[c, d],
            sect=dest,
        )

    def return_arrival(c, d, batch):
        sender = (s - d + S) % S
        return remote(
            ret_out.at[batch, pair_slots(sender), chunk(c)],
            ret_in.at[batch, pair_slots(sender), chunk(c)],
            ret_send.at[c, d],
            ret_recv.at[c, d],
            sect=sender,
        )

    for batch in range(2):
        for c in range(NC):
            each_partner(S, batch, lambda d: dispatch_arrival(c, d, batch).wait_recv())
            share_copy(c, t, batch).start()
            accumulate(c, t, batch, first=c == 0)
            if c > 0:
                share_copy(c - 1, 1 - t, batch).wait_recv()
                accumulate(c - 1, 1 - t, batch)
        share_copy(NC - 1, 1 - t, batch).wait_recv()
        accumulate(NC - 1, 1 - t, batch)

        gate_value = acc[0]
        act[...] = (gate_value / (1.0 + jnp.exp(-gate_value)) * acc[1]).astype(bf16)
        if batch == 0:
            copies[3].wait()
        for c in range(NC):
            cols = slice(back_starts[c], back_starts[c] + back[c])
            down_out[batch, :, cols] = jnp.dot(
                act[...], wd[:, columns(1 - t, NC - 1 - c)], preferred_element_type=f32
            ).astype(bf16)
            down_copy(c, batch).start()
        for c in range(NC):
            cols = slice(back_starts[c], back_starts[c] + back[c])
            own = jnp.dot(
                act[...], wd[:, columns(t, NC - 1 - c)], preferred_element_type=f32
            ).astype(bf16)
            down_copy(c, batch).wait_recv()
            ret_out[batch, :, cols] = (
                own.astype(f32) + down_in[batch, :, cols].astype(f32)
            ).astype(bf16)
            each_partner(S, batch, lambda d: return_copy(c, d, batch).start())
            if batch == 0:
                ret_in[0, pair_slots(s), cols] = ret_out[0, pair_slots(s), cols]

    remote(
        attended.at[their_half, my_columns],
        attended.at[their_half, my_columns],
        nx_send.at[1],
        nx_recv.at[1],
        tp=1 - t,
    ).wait_recv()
    for batch in range(2):
        mix = mixing[(s + batch) % 2]
        mix_high = mix.astype(bf16)
        rest = mix - mix_high.astype(f32)
        mix_mid = rest.astype(bf16)
        mix_low = (rest - mix_mid.astype(f32)).astype(bf16)
        for c in range(NC):
            cols = slice(back_starts[c], back_starts[c] + back[c])
            each_partner(S, batch, lambda d: return_arrival(c, d, batch).wait_recv())
            got = ret_in[batch, :, cols]
            expert_sum = (
                jnp.dot(mix_high, got, preferred_element_type=f32)
                + jnp.dot(mix_mid, got, preferred_element_type=f32)
                + jnp.dot(mix_low, got, preferred_element_type=f32)
            )
            total = attended[:, columns(t, NC - 1 - c)] + expert_sum
            if batch == 0:
                attended[:, columns(t, NC - 1 - c)] = total
            else:
                out[:, cols] = total.astype(bf16)

    for k in range(1, ring_half + 1):
        for direction, h in ring_pairs:
            ring_copy(k, direction, h).wait_send()
    for o in range(S):
        exchange(o).wait_send()
        if o > 0:
            feature_copy(o).wait_send()
    normed_copy.wait_send()
    att_copy.wait_send()
    for c in range(NC):
        for batch in range(2):
            each_partner(S, batch, lambda d: dispatch_copy(c, d, batch).wait_send())
            share_copy(c, t, batch).wait_send()
            down_copy(c, batch).wait_send()
            each_partner(S, batch, lambda d: return_copy(c, d, batch).wait_send())


def chunk_widths(total):
    unit = 256 if total % 256 == 0 else 128
    units = total // unit
    widths = [2 * unit] * (units // 2)
    return tuple(widths + [unit] * (units % 2))


def layer_call(S, lengths, home, q, k, v, wo_t, resid, gain, chosen, probs, gate_up, down_proj):
    f32, bf16 = jnp.float32, jnp.bfloat16
    rows, heads_count, head_dim = q.shape
    half = rows // 2
    F = wo_t.shape[0]
    D = F * S
    hidden = down_proj.shape[0]
    slots = S * (rows // CAP_SHARE)
    widths = chunk_widths(D // 2)
    NC = len(widths)
    dma = pltpu.SemaphoreType.DMA
    vmem = pl.BlockSpec(memory_space=pltpu.VMEM)
    smem = pl.BlockSpec(memory_space=pltpu.SMEM)
    hbm = pl.BlockSpec(memory_space=pl.ANY)
    return pl.pallas_call(
        functools.partial(layer_kernel, S, widths),
        out_shape=pltpu.VMEM((rows, D // 2), bf16),
        in_specs=[smem, smem, hbm, hbm, hbm, hbm, vmem, vmem, vmem, vmem, hbm, hbm],
        out_specs=vmem,
        scratch_shapes=[
            pltpu.VMEM(q.shape, bf16),
            pltpu.VMEM(k.shape, bf16),
            pltpu.VMEM(v.shape, bf16),
            pltpu.VMEM(wo_t.shape, bf16),
            pltpu.VMEM(gate_up.shape, bf16),
            pltpu.VMEM(down_proj.shape, bf16),
            pltpu.VMEM((rows * heads_count, head_dim), f32),
            pltpu.VMEM((S * rows, heads_count * head_dim), bf16),
            pltpu.VMEM((S, 2, half, F), f32),
            pltpu.VMEM((S, half, F), f32),
            pltpu.VMEM((S, half, F), bf16),
            pltpu.VMEM((S, half, F), bf16),
            pltpu.VMEM((rows, D), bf16),
            pltpu.VMEM((rows, D), f32),
            pltpu.VMEM((slots, rows), bf16),
            pltpu.VMEM((2, rows, slots // 2), f32),
            pltpu.VMEM((slots, D // 2), bf16),
            pltpu.VMEM((2, slots // 2, D), bf16),
            pltpu.VMEM((2, slots // 2, hidden), f32),
            pltpu.VMEM((slots // 2, hidden), bf16),
            pltpu.VMEM((2, slots // 2, D // 2), bf16),
            pltpu.VMEM((2, slots // 2, D // 2), bf16),
            pltpu.VMEM((2, slots // 2, D // 2), bf16),
            pltpu.VMEM((2, slots // 2, D // 2), bf16),
            dma((3, 2)),
            dma((4,)),
            dma((2, S // 2, 2)),
            dma((2, S // 2, 2)),
            dma((S,)),
            dma((S,)),
            dma((S,)),
            dma((S,)),
            dma((2,)),
            dma((2,)),
            dma((NC, S)),
            dma((NC, S)),
            dma((2, NC)),
            dma((2, NC)),
            dma((2, NC)),
            dma((2, NC)),
            dma((NC, S)),
            dma((NC, S)),
        ],
        compiler_params=pltpu.CompilerParams(
            collective_id=0, has_side_effects=True, vmem_limit_bytes=60 * 1024 * 1024
        ),
        cost_estimate=pl.CostEstimate(
            flops=2 * S * rows * wo_t.size + 6 * slots * D * hidden,
            bytes_accessed=2 * (wo_t.size + gate_up.size + down_proj.size),
            transcendentals=slots * hidden,
        ),
    )(lengths, home, q, k, v, wo_t, resid, gain, chosen, probs, gate_up, down_proj)


def body(
    queries,
    keys,
    values,
    kv_lengths,
    out_proj,
    resid,
    norm_gain,
    experts_chosen,
    route_probs,
    expert_home,
    gate_up,
    down_proj,
):
    row_count, context, _, head_dim = keys.shape
    return layer_call(
        lax.axis_size("sect"),
        kv_lengths,
        expert_home,
        queries,
        keys.reshape(row_count, context, head_dim),
        values.reshape(row_count, context, head_dim),
        out_proj.T,
        resid,
        norm_gain,
        experts_chosen.T,
        route_probs.T,
        gate_up,
        down_proj,
    )


def solution(mesh):
    in_specs = (
        P(("groups", "sect"), "tp", None),
        P(("groups", "sect"), None, "tp", None),
        P(("groups", "sect"), None, "tp", None),
        P(("groups", "sect")),
        P("tp", "sect"),
        P(("groups", "sect"), None),
        P(),
        P(("groups", "sect"), None),
        P(("groups", "sect"), None),
        P(),
        P(None, None, ("sect", "tp")),
        P(("sect", "tp"), None),
    )
    out_specs = P(("groups", "sect"), "tp")
    return jax.shard_map(body, mesh=mesh, in_specs=in_specs, out_specs=out_specs, check_vma=False)
```
